32 devices in a mesh: gx: 4 (over x, core), yz: 8 (over z, y).
Axes of the slice: x: 2, y: 2, z: 4, core: 2. Of those that a mesh axis runs over, the one named last changes fastest.
Arguments:
- hidden_in: bfloat16 [2, 32, 8192], P(None, ('gx', 'yz')), may hold values from -6 to 6
- k_cache: bfloat16 [32, 1024, 1024], P(('gx', 'yz'))
- v_cache: bfloat16 [32, 1024, 1024], P(('gx', 'yz')), may hold values from -6 to 6
- lengths: int32 [32], P(('gx', 'yz')), may hold values from 1 to 1024, as said below
- counts: int32 [32, 16], P(('gx', 'yz')), may hold values from 0 to 3
- token_elem: int32 [512], replicated, may hold values from 0 to 16, as said below
- tokens: int32 [32], P(('gx', 'yz')), may hold values from 0 to 511
- attn_gain: float32 [8192], replicated, may hold values from 0.5 to 1.5
- qkv_weight: bfloat16 [8192, 10240], P('gx', 'yz'), may hold values from -0.0625 to 0.0625
- o_weight: bfloat16 [8192, 8192], P('gx', 'yz'), may hold values from -0.0625 to 0.0625
- ffn_gain: float32 [8192], replicated, may hold values from 0.5 to 1.5
- gate_up_weight: bfloat16 [8192, 57344], P('gx', 'yz'), may hold values from -0.0625 to 0.0625
- down_weight: bfloat16 [28672, 8192], P('gx', 'yz'), may hold values from -0.03125 to 0.03125
- final_gain: float32 [8192], replicated, may hold values from 0.5 to 1.5
- lm_weight: bfloat16 [8192, 512], P(('gx', 'yz'))
Outputs:
- layer_out: bfloat16 [2, 32, 8192], P(None, ('gx', 'yz'))
- log_probs: float32 [2, 32, 512], P(None, ('gx', 'yz'))
The draws below stay inside these ranges and needn't reach their ends.
Inputs may be any that keep to these rules, and one draw needn't show every extreme that they name: `lengths`: some spectrum uses all 1024 positions. `token_elem`: some token has no element (value 16).
All inputs are finite; a program needn't handle non-finite values.
Results may differ from the reference program's by a relative error of at most 0.022.
Values may be sent and summed in bfloat16 or wider, within the bound.
A program may use at most 128 MiB of HBM per device.

```python
import math
import jax
import jax.numpy as jnp
from jax import lax

D = 8192
FF = 28672
HEADS = 64
KV_HEADS = 8
HEAD = 128
VOCAB = 512
ELEMENTS = 16
CACHE = 1024
BATCH = 32


def draw_k_cache(key, part):
    base_key = jax.random.fold_in(key, 0)
    values = jax.random.normal(base_key, (BATCH, CACHE, KV_HEADS * HEAD), jnp.float32)
    return values.astype(jnp.bfloat16)


def draw_lm_weight(key, part):
    base_key = jax.random.fold_in(key, 0)
    values = jax.random.normal(base_key, (D, VOCAB), jnp.float32) * (3.0 / math.sqrt(D))
    return values.astype(jnp.bfloat16)


def draw_lengths(key, part):
    base_key, pick_key = jax.random.split(key)
    drawn = jax.random.randint(base_key, (BATCH,), 1, CACHE + 1)
    target = jax.random.randint(pick_key, (), 0, BATCH)
    return drawn.at[target].set(CACHE).astype(jnp.int32)


def draw_token_elem(key, part):
    base_key, pick_key = jax.random.split(key)
    drawn = jax.random.randint(base_key, (VOCAB,), 0, ELEMENTS + 1)
    target = jax.random.randint(pick_key, (), 0, VOCAB)
    return drawn.at[target].set(ELEMENTS).astype(jnp.int32)


def plant(array, key, least, high):
    longest = array.shape.index(max(array.shape))
    spots = []
    for shift in (0, 1):
        where = [jax.random.randint(jax.random.fold_in(key, axis), (), 0, length) for axis, length in enumerate(array.shape)]
        where[longest] = (where[longest] + shift) % array.shape[longest]
        spots.append(tuple(where))
    return array.at[spots[0]].set(least).at[spots[1]].set(high)


def block_levels(key, dims, cuts, smallest, high):
    def one(dim, blocks):
        draws = jax.random.uniform(jax.random.fold_in(jax.random.fold_in(key, 6), dim), (blocks,), jnp.float32, smallest / len(cuts), high / len(cuts))
        return jnp.repeat(jnp.exp(draws), dims[dim] // blocks).reshape((-1,) + (1,) * (len(dims) - dim - 1))

    level = one(*cuts[0])
    for cut in cuts[1:]:
        level = level * one(*cut)
    return level


def bell_draw(rng, shape, scale, bound, cuts=(), held_as=jnp.bfloat16):
    array = scale * jax.random.normal(rng, shape, jnp.float32)
    if cuts:
        array = array * block_levels(rng, shape, cuts, -0.22, 0.18)
    return jnp.clip(array, -bound, bound).astype(held_as)


def setup_inputs(seed: int = 0) -> dict:
    splits = jax.random.split(jax.random.key(seed), 16)
    return {
        "hidden_in": bell_draw(splits[0], (2, BATCH, D), 1.0, 6.0, ((1, 32),)),
        "k_cache": draw_k_cache(jax.random.fold_in(splits[15], 71), 0),
        "v_cache": bell_draw(splits[2], (BATCH, CACHE, KV_HEADS * HEAD), 1.0, 6.0, ((0, 32),)),
        "lengths": draw_lengths(jax.random.fold_in(splits[15], 71), 0),
        "counts": plant(jax.random.randint(splits[4], (BATCH, ELEMENTS), 0, 4), jax.random.fold_in(splits[4], 1), 0, 3).astype(jnp.int32),
        "token_elem": draw_token_elem(jax.random.fold_in(splits[15], 71), 0),
        "tokens": plant(jax.random.randint(splits[6], (BATCH,), 0, VOCAB), jax.random.fold_in(splits[6], 1), 0, VOCAB - 1).astype(jnp.int32),
        "attn_gain": jnp.clip(1.0 + 0.1 * jax.random.normal(splits[7], (D,), jnp.float32), 0.5, 1.5),
        "qkv_weight": bell_draw(splits[8], (D, D + 2 * KV_HEADS * HEAD), D ** -0.5, 0.0625, ((0, 4), (1, 8))),
        "o_weight": bell_draw(splits[9], (HEADS * HEAD, D), (HEADS * HEAD) ** -0.5, 0.0625, ((0, 4), (1, 8))),
        "ffn_gain": jnp.clip(1.0 + 0.1 * jax.random.normal(splits[10], (D,), jnp.float32), 0.5, 1.5),
        "gate_up_weight": bell_draw(splits[11], (D, 2 * FF), D ** -0.5, 0.0625, ((0, 4), (1, 8))),
        "down_weight": bell_draw(splits[12], (FF, D), FF ** -0.5, 0.03125, ((0, 4), (1, 8))),
        "final_gain": jnp.clip(1.0 + 0.1 * jax.random.normal(splits[13], (D,), jnp.float32), 0.5, 1.5),
        "lm_weight": draw_lm_weight(jax.random.fold_in(splits[15], 71), 0),
    }


NORM_EPS = 1e-05
ROPE_THETA = 500000.0

def norm_rows(values, gain_vec):
    wide = values.astype(jnp.float32)
    inverse = lax.rsqrt(lax.optimization_barrier(jnp.mean(wide * wide, axis=-1, keepdims=True)) + NORM_EPS)
    return (wide * inverse * gain_vec.astype(jnp.float32)).astype(jnp.bfloat16)

def rotate(heads_in, positions):
    half_width = heads_in.shape[-1] // 2
    frequency = jnp.power(ROPE_THETA, -(jnp.arange(half_width, dtype=jnp.float32) * 2.0 / heads_in.shape[-1]))
    angles = positions.astype(jnp.float32)[:, None] * frequency[None, :]
    cos_part = jnp.cos(angles)[:, None, :]
    sin_part = jnp.sin(angles)[:, None, :]
    wide = heads_in.astype(jnp.float32)
    first_half = wide[..., :half_width]
    second_half = wide[..., half_width:]
    joined = jnp.concatenate([first_half * cos_part - second_half * sin_part, second_half * cos_part + first_half * sin_part], -1)
    return joined.astype(jnp.bfloat16)

def attention(queries, k_cache, v_cache, lengths, keys_new, values_new):
    groups = HEADS // KV_HEADS
    factor = 1.0 / math.sqrt(HEAD)

    def per_row(row_items):
        query_row, kcache_row, vcache_row, length_row, knew_row, vnew_row = row_items
        query_wide = query_row.astype(jnp.float32).reshape(KV_HEADS, groups, HEAD)
        kcache_wide = kcache_row.astype(jnp.float32).reshape(CACHE, KV_HEADS, HEAD)
        vcache_wide = vcache_row.astype(jnp.float32).reshape(CACHE, KV_HEADS, HEAD)
        scores_cache = jnp.einsum('kgd,lkd->kgl', query_wide, kcache_wide) * factor
        valid = (jnp.arange(CACHE) < length_row)[None, None, :]
        scores_cache = jnp.where(valid, scores_cache, -jnp.inf)
        scores_new = jnp.einsum('kgd,nkd->kgn', query_wide, knew_row.astype(jnp.float32)) * factor
        largest = jnp.maximum(lax.optimization_barrier(jnp.max(scores_cache, -1)), lax.optimization_barrier(jnp.max(scores_new, -1)))[..., None]
        exp_cache = jnp.where(valid, jnp.exp(scores_cache - largest), 0.0)
        exp_new = jnp.exp(scores_new - largest)
        denominator = lax.optimization_barrier(jnp.sum(exp_cache, -1, keepdims=True)) + lax.optimization_barrier(jnp.sum(exp_new, -1, keepdims=True))
        weights_cache = (exp_cache / denominator).astype(jnp.bfloat16)
        weights_new = (exp_new / denominator).astype(jnp.bfloat16)
        result = jnp.einsum('kgl,lkd->kgd', weights_cache.astype(jnp.float32), vcache_wide)
        result = result + jnp.einsum('kgn,nkd->kgd', weights_new.astype(jnp.float32), vnew_row.astype(jnp.float32))
        return result.reshape(HEADS * HEAD).astype(jnp.bfloat16)
    return lax.map(per_row, (queries, k_cache, v_cache, lengths, keys_new, values_new))

def element_table(token_elem):
    return (token_elem[:, None] == jnp.arange(ELEMENTS, dtype=jnp.int32)[None, :]).astype(jnp.float32)

def masked_log_probs(logits, remaining, token_elem):
    element_hot = element_table(token_elem)
    per_token = jnp.dot(remaining, element_hot.T)
    allowed = (per_token > 0.5) | (token_elem == ELEMENTS)[None, :]
    largest = lax.optimization_barrier(jnp.max(jnp.where(allowed, logits, -jnp.inf), -1, keepdims=True))
    shifted = logits - largest
    denominator = lax.optimization_barrier(jnp.sum(jnp.where(allowed, jnp.exp(shifted), 0.0), -1, keepdims=True))
    return jnp.where(allowed, shifted - jnp.log(denominator), 0.0)

def used_elements(tokens, token_elem):
    token_hot = (tokens[:, None] == jnp.arange(VOCAB, dtype=jnp.int32)[None, :]).astype(jnp.float32)
    return jnp.dot(token_hot, element_table(token_elem))

def reference(hidden_in, k_cache, v_cache, lengths, counts, token_elem, tokens, attn_gain, qkv_weight, o_weight, ffn_gain, gate_up_weight, down_weight, final_gain, lm_weight):
    q_width = HEADS * HEAD
    kv_width = KV_HEADS * HEAD
    key_list = []
    value_list = []
    result_list = []
    log_list = []
    remaining = counts.astype(jnp.float32)
    for which_step in range(2):
        layer_in = hidden_in[which_step]
        normed = norm_rows(layer_in, attn_gain)
        mixed = jnp.dot(normed, qkv_weight, preferred_element_type=jnp.float32).astype(jnp.bfloat16)
        positions = lengths + which_step
        queries = rotate(mixed[:, :q_width].reshape(BATCH, HEADS, HEAD), positions)
        keys_now = rotate(mixed[:, q_width:q_width + kv_width].reshape(BATCH, KV_HEADS, HEAD), positions)
        values_now = mixed[:, q_width + kv_width:].reshape(BATCH, KV_HEADS, HEAD)
        key_list.append(keys_now)
        value_list.append(values_now)
        attended = attention(queries, k_cache, v_cache, lengths, jnp.stack(key_list, 1), jnp.stack(value_list, 1))
        projected = jnp.dot(attended, o_weight, preferred_element_type=jnp.float32).astype(jnp.bfloat16)
        residual = (layer_in.astype(jnp.float32) + projected.astype(jnp.float32)).astype(jnp.bfloat16)
        gate_up = jnp.dot(norm_rows(residual, ffn_gain), gate_up_weight, preferred_element_type=jnp.float32).astype(jnp.bfloat16)
        hidden_units = (jax.nn.silu(gate_up[:, :FF].astype(jnp.float32)) * gate_up[:, FF:].astype(jnp.float32)).astype(jnp.bfloat16)
        lowered = jnp.dot(hidden_units, down_weight, preferred_element_type=jnp.float32).astype(jnp.bfloat16)
        result = (residual.astype(jnp.float32) + lowered.astype(jnp.float32)).astype(jnp.bfloat16)
        logits = jnp.dot(norm_rows(result, final_gain), lm_weight, preferred_element_type=jnp.float32)
        log_list.append(masked_log_probs(logits, remaining, token_elem))
        result_list.append(result)
        remaining = remaining - used_elements(tokens, token_elem)
    return (jnp.stack(result_list), jnp.stack(log_list))
```

```python
import math

import jax
import jax.numpy as jnp
from jax import lax
from jax.sharding import PartitionSpec as P

FF = 28672
HEADS = 64
KV_HEADS = 8
HEAD = 128
VOCAB = 512
ELEMENTS = 16


NORM_EPS = 1e-05
ROPE_THETA = 500000.0


def norm_rows(values, gain_vec):
    wide = values.astype(jnp.float32)
    inverse = lax.rsqrt(jnp.mean(wide * wide, axis=-1, keepdims=True) + NORM_EPS)
    return (wide * inverse * gain_vec).astype(jnp.bfloat16)


def rotate(heads_in, positions):
    half_width = heads_in.shape[-1] // 2
    frequency = jnp.power(
        ROPE_THETA, -(jnp.arange(half_width, dtype=jnp.float32) * 2.0 / heads_in.shape[-1])
    )
    angles = positions.astype(jnp.float32)[:, None] * frequency[None, :]
    cos_part = jnp.cos(angles)[:, None, :]
    sin_part = jnp.sin(angles)[:, None, :]
    wide = heads_in.astype(jnp.float32)
    first_half = wide[..., :half_width]
    second_half = wide[..., half_width:]
    joined = jnp.concatenate(
        [
            first_half * cos_part - second_half * sin_part,
            second_half * cos_part + first_half * sin_part,
        ],
        -1,
    )
    return joined.astype(jnp.bfloat16)


def spread_rows(inputs):
    gathered = lax.all_gather(inputs, "yz", axis=0, tiled=True)
    return lax.all_to_all(gathered, "gx", split_axis=1, concat_axis=0, tiled=True)


def project(inputs, weight):
    spread = spread_rows(inputs)
    summed = lax.psum_scatter(
        jnp.dot(spread, weight, preferred_element_type=jnp.float32),
        "gx",
        scatter_dimension=0,
        tiled=True,
    )
    return lax.all_to_all(
        summed.astype(jnp.bfloat16), "yz", split_axis=0, concat_axis=1, tiled=True
    )


def head_logits(normed, lm_weight):
    slice_width = lm_weight.shape[0]
    offset_cols = lax.axis_index("yz") * slice_width
    spread = spread_rows(normed)
    own_cols = lax.dynamic_slice_in_dim(spread, offset_cols, slice_width, 1)
    return lax.psum_scatter(
        jnp.dot(own_cols, lm_weight, preferred_element_type=jnp.float32),
        ("gx", "yz"),
        scatter_dimension=0,
        tiled=True,
    )


def attend(queries, k_cache, v_cache, lengths, keys_new, values_new):
    groups = HEADS // KV_HEADS
    factor = 1.0 / math.sqrt(HEAD)
    steps, rows_here = queries.shape[:2]
    cache_len = k_cache.shape[1]
    query_heads = queries.reshape(steps, rows_here, KV_HEADS, groups, HEAD)
    kcache_heads = k_cache.reshape(rows_here, cache_len, KV_HEADS, HEAD)
    vcache_heads = v_cache.reshape(rows_here, cache_len, KV_HEADS, HEAD)
    knew_heads = keys_new.reshape(steps, rows_here, KV_HEADS, HEAD)
    vnew_heads = values_new.reshape(steps, rows_here, KV_HEADS, HEAD)
    scores_cache = (
        jnp.einsum("srkgd,rlkd->srkgl", query_heads, kcache_heads, preferred_element_type=jnp.float32)
        * factor
    )
    valid = jnp.arange(cache_len)[None, None, None, None, :] < lengths[None, :, None, None, None]
    scores_cache = jnp.where(valid, scores_cache, -jnp.inf)
    scores_new = (
        jnp.einsum("srkgd,nrkd->srkgn", query_heads, knew_heads, preferred_element_type=jnp.float32)
        * factor
    )
    order = jnp.arange(steps)
    seen = (order[None, :] <= order[:, None])[:, None, None, None, :]
    scores_new = jnp.where(seen, scores_new, -jnp.inf)
    largest = jnp.maximum(jnp.max(scores_cache, -1), jnp.max(scores_new, -1))[..., None]
    exp_cache = jnp.where(valid, jnp.exp(scores_cache - largest), 0.0)
    exp_new = jnp.where(seen, jnp.exp(scores_new - largest), 0.0)
    denominator = jnp.sum(exp_cache, -1, keepdims=True) + jnp.sum(exp_new, -1, keepdims=True)
    weights_cache = (exp_cache / denominator).astype(jnp.bfloat16)
    weights_new = (exp_new / denominator).astype(jnp.bfloat16)
    result = jnp.einsum(
        "srkgl,rlkd->srkgd", weights_cache, vcache_heads, preferred_element_type=jnp.float32
    )
    result = result + jnp.einsum(
        "srkgn,nrkd->srkgd", weights_new, vnew_heads, preferred_element_type=jnp.float32
    )
    return result.reshape(steps * rows_here, HEADS * HEAD).astype(jnp.bfloat16)


def element_table(token_elem):
    return (token_elem[:, None] == jnp.arange(ELEMENTS, dtype=jnp.int32)[None, :]).astype(
        jnp.float32
    )


def masked_log_probs(logits, remaining, token_elem):
    element_hot = element_table(token_elem)
    per_token = jnp.dot(remaining, element_hot.T)
    allowed = (per_token > 0.5) | (token_elem == ELEMENTS)[None, :]
    largest = jnp.max(jnp.where(allowed, logits, -jnp.inf), -1, keepdims=True)
    shifted = logits - largest
    denominator = jnp.sum(jnp.where(allowed, jnp.exp(shifted), 0.0), -1, keepdims=True)
    return jnp.where(allowed, shifted - jnp.log(denominator), 0.0)


def used_elements(tokens, token_elem):
    token_hot = (tokens[:, None] == jnp.arange(VOCAB, dtype=jnp.int32)[None, :]).astype(jnp.float32)
    return jnp.dot(token_hot, element_table(token_elem))


def per_device(
    hidden_in,
    k_cache,
    v_cache,
    lengths,
    counts,
    token_elem,
    tokens,
    attn_gain,
    qkv_weight,
    o_weight,
    ffn_gain,
    gate_up_weight,
    down_weight,
    final_gain,
    lm_weight,
):
    q_width = HEADS * HEAD
    kv_width = KV_HEADS * HEAD
    steps, rows_here, width = hidden_in.shape
    layer_in = hidden_in.reshape(steps * rows_here, width)
    positions = (jnp.arange(steps, dtype=jnp.int32)[:, None] + lengths[None, :]).reshape(-1)
    mixed = project(norm_rows(layer_in, attn_gain), qkv_weight)
    queries = rotate(mixed[:, :q_width].reshape(-1, HEADS, HEAD), positions)
    keys_now = rotate(
        mixed[:, q_width : q_width + kv_width].reshape(-1, KV_HEADS, HEAD), positions
    )
    values_now = mixed[:, q_width + kv_width :]
    attended = attend(
        queries.reshape(steps, rows_here, q_width),
        k_cache,
        v_cache,
        lengths,
        keys_now.reshape(steps, rows_here, kv_width),
        values_now.reshape(steps, rows_here, kv_width),
    )
    projected = project(attended, o_weight)
    residual = (layer_in.astype(jnp.float32) + projected.astype(jnp.float32)).astype(jnp.bfloat16)
    gate_up = project(norm_rows(residual, ffn_gain), gate_up_weight)
    hidden_units = (
        jax.nn.silu(gate_up[:, :FF].astype(jnp.float32)) * gate_up[:, FF:].astype(jnp.float32)
    ).astype(jnp.bfloat16)
    lowered = project(hidden_units, down_weight)
    result = (residual.astype(jnp.float32) + lowered.astype(jnp.float32)).astype(jnp.bfloat16)
    logits = head_logits(norm_rows(result, final_gain), lm_weight)
    logit_steps = logits.reshape(steps, rows_here, VOCAB)
    outputs = result.reshape(steps, rows_here, width)
    remaining = counts.astype(jnp.float32)
    first_log = masked_log_probs(logit_steps[0], remaining, token_elem)
    remaining = remaining - used_elements(tokens, token_elem)
    second_log = masked_log_probs(logit_steps[1], remaining, token_elem)
    return (outputs, jnp.stack([first_log, second_log]))


def solution(mesh):
    return jax.shard_map(
        per_device,
        mesh=mesh,
        in_specs=(
            P(None, ("gx", "yz"), None),
            P(("gx", "yz"), None, None),
            P(("gx", "yz"), None, None),
            P(("gx", "yz")),
            P(("gx", "yz"), None),
            P(),
            P(("gx", "yz")),
            P(),
            P("gx", "yz"),
            P("gx", "yz"),
            P(),
            P("gx", "yz"),
            P("gx", "yz"),
            P(),
            P(("gx", "yz"), None),
        ),
        out_specs=(P(None, ("gx", "yz"), None), P(None, ("gx", "yz"), None)),
        check_vma=False,
    )
```

```python
import functools
import math

import jax
import jax.numpy as jnp
from jax import lax
from jax.experimental import pallas as pl
from jax.experimental.pallas import tpu as pltpu
from jax.sharding import PartitionSpec as P

FF = 28672
HEADS = 64
KV_HEADS = 8
HEAD = 128
VOCAB = 512
ELEMENTS = 16


NORM_EPS = 1e-05
ROPE_THETA = 500000.0


def norm_rows(values, gain_vec):
    wide = values.astype(jnp.float32)
    inverse = lax.rsqrt(jnp.mean(wide * wide, axis=-1, keepdims=True) + NORM_EPS)
    return (wide * inverse * gain_vec).astype(jnp.bfloat16)


def rotate(heads_in, positions):
    half_width = heads_in.shape[-1] // 2
    frequency = jnp.power(
        ROPE_THETA, -(jnp.arange(half_width, dtype=jnp.float32) * 2.0 / heads_in.shape[-1])
    )
    angles = positions.astype(jnp.float32)[:, None] * frequency[None, :]
    cos_part = jnp.cos(angles)[:, None, :]
    sin_part = jnp.sin(angles)[:, None, :]
    wide = heads_in.astype(jnp.float32)
    first_half = wide[..., :half_width]
    second_half = wide[..., half_width:]
    joined = jnp.concatenate(
        [
            first_half * cos_part - second_half * sin_part,
            second_half * cos_part + first_half * sin_part,
        ],
        -1,
    )
    return joined.astype(jnp.bfloat16)


def project_kernel(
    nx,
    ny,
    head,
    tile,
    x_ref,
    w_ref,
    out_ref,
    wbuf,
    x1,
    strips,
    slot,
    xall,
    xmat,
    pbuf,
    rbuf,
    sbuf,
    obuf,
    wsem,
    ssem1,
    rsem1,
    ssem2,
    rsem2,
    ssem3,
    rsem3,
    ssem4,
    rsem4,
):
    gx = lax.axis_index("gx")
    yz = lax.axis_index("yz")
    count = wbuf.shape[0]
    rows = x1.shape[1]
    mesh_id = pl.DeviceIdType.MESH

    def fetch(c):
        cols = pl.ds(pl.multiple_of(c * tile, tile), tile)
        return pltpu.make_async_copy(w_ref.at[:, cols], wbuf.at[c], wsem.at[c])

    def begin(c, carry):
        fetch(c).start()
        return carry

    lax.fori_loop(0, count, begin, 0)

    home = yz // 2
    barrier = pltpu.get_barrier_semaphore()
    for d in range(1, nx):
        pl.semaphore_signal(
            barrier, inc=1, device_id=(lax.rem(gx + d, nx), yz), device_id_type=mesh_id
        )
    for d in range(1, ny):
        pl.semaphore_signal(
            barrier, inc=1, device_id=(gx, lax.rem(yz + d, ny)), device_id_type=mesh_id
        )
    for jj in range(ny):
        @pl.when(jnp.logical_not((home == gx) & (yz == jj)))
        def _():
            pl.semaphore_signal(barrier, inc=1, device_id=(home, jj), device_id_type=mesh_id)
    apart = (lax.rem(home + nx - gx, nx) + nx - 2) // (nx - 1)
    pl.semaphore_wait(barrier, nx - 1 + ny - 1 + ny - 1 + apart)

    def first(d):
        to = lax.rem(gx + d, nx)
        return pltpu.make_async_remote_copy(
            src_ref=x_ref.at[to],
            dst_ref=x1.at[gx],
            send_sem=ssem1.at[d],
            recv_sem=rsem1.at[d],
            device_id=(to, yz),
            device_id_type=mesh_id,
        )

    def first_in(d):
        return pltpu.make_async_remote_copy(
            src_ref=x_ref.at[gx],
            dst_ref=x1.at[lax.rem(gx + nx - d, nx)],
            send_sem=ssem1.at[d],
            recv_sem=rsem1.at[d],
            device_id=(lax.rem(gx + d, nx), yz),
            device_id_type=mesh_id,
        )

    for d in range(1, nx):
        first(d).start()
    x1[gx] = x_ref[gx]
    for d in range(1, nx):
        first_in(d).wait_recv()
    for g in range(nx):
        strips[g * rows : (g + 1) * rows, :] = x1[g].astype(jnp.float32)
    if head:
        width = xmat.shape[1]
        for jj in range(ny):
            slot[jj] = strips[:, jj * width : (jj + 1) * width].astype(jnp.bfloat16)
        xall[yz] = slot[yz]
    else:
        slot[0] = strips[...].astype(jnp.bfloat16)
        xall[yz] = slot[0]

    def second(d):
        to = lax.rem(yz + d, ny)
        return pltpu.make_async_remote_copy(
            src_ref=slot.at[to] if head else slot.at[0],
            dst_ref=xall.at[yz],
            send_sem=ssem2.at[d],
            recv_sem=rsem2.at[d],
            device_id=(gx, to),
            device_id_type=mesh_id,
        )

    def second_in(d):
        return pltpu.make_async_remote_copy(
            src_ref=slot.at[0],
            dst_ref=xall.at[lax.rem(yz + ny - d, ny)],
            send_sem=ssem2.at[d],
            recv_sem=rsem2.at[d],
            device_id=(gx, lax.rem(yz + d, ny)),
            device_id_type=mesh_id,
        )

    for d in range(1, ny):
        second(d).start()
    for d in range(1, ny):
        second_in(d).wait_recv()
    group = 2 * nx * rows
    for t in range(ny // 2):
        xmat[t * group : (t + 1) * group, :] = jnp.concatenate(
            [xall[2 * t].astype(jnp.float32), xall[2 * t + 1].astype(jnp.float32)], 0
        ).astype(jnp.bfloat16)

    def third(c, d):
        cols = pl.ds(pl.multiple_of(c * tile, tile), tile)
        to = lax.rem(gx + d, nx)
        return pltpu.make_async_remote_copy(
            src_ref=pbuf.at[to, :, cols],
            dst_ref=rbuf.at[d, :, cols],
            send_sem=ssem3.at[c, d],
            recv_sem=rsem3.at[c, d],
            device_id=(to, yz),
            device_id_type=mesh_id,
        )

    def multiply(c, carry):
        cols = pl.ds(pl.multiple_of(c * tile, tile), tile)
        fetch(c).wait()
        product = jnp.dot(xmat[...], wbuf[c], preferred_element_type=jnp.float32)
        for t in range(nx):
            pbuf[t, :, cols] = product[t * group : (t + 1) * group].astype(pbuf.dtype)
        for d in range(1, nx):
            third(c, d).start()
        return carry

    lax.fori_loop(0, count, multiply, 0)

    def reduce(c, carry):
        cols = pl.ds(pl.multiple_of(c * tile, tile), tile)
        for d in range(1, nx):
            third(c, d).wait_recv()
        total = pbuf[gx, :, cols].astype(jnp.float32)
        for d in range(1, nx):
            total = total + rbuf[d, :, cols].astype(jnp.float32)
        for k in range(2 * nx):
            sbuf[k, :, cols] = total[k * rows : (k + 1) * rows].astype(sbuf.dtype)
        return carry

    lax.fori_loop(0, count, reduce, 0)

    def fourth(k, u, g):
        return pltpu.make_async_remote_copy(
            src_ref=sbuf.at[k],
            dst_ref=obuf.at[yz],
            send_sem=ssem4.at[k],
            recv_sem=rsem4.at[yz],
            device_id=(g, 2 * gx + u),
            device_id_type=mesh_id,
        )

    def fourth_in(jj):
        return pltpu.make_async_remote_copy(
            src_ref=sbuf.at[0],
            dst_ref=obuf.at[jj],
            send_sem=ssem4.at[0],
            recv_sem=rsem4.at[jj],
            device_id=(lax.rem(gx + 1, nx), yz),
            device_id_type=mesh_id,
        )

    for u in range(2):
        for g in range(nx):
            mine = (gx == g) & (yz == 2 * gx + u)

            @pl.when(jnp.logical_not(mine))
            def _():
                fourth(u * nx + g, u, g).start()

            @pl.when(mine)
            def _():
                obuf[yz] = sbuf[u * nx + g]

    for jj in range(ny):
        @pl.when(jnp.logical_not((home == gx) & (yz == jj)))
        def _():
            fourth_in(jj).wait_recv()
    if head:
        out_ref[...] = sum(obuf[jj] for jj in range(ny))
    else:
        size = obuf.shape[2]
        for jj in range(ny):
            out_ref[:, jj * size : (jj + 1) * size] = obuf[jj]

    for d in range(1, nx):
        first(d).wait_send()
    for d in range(1, ny):
        second(d).wait_send()

    def drain(c, carry):
        for d in range(1, nx):
            third(c, d).wait_send()
        return carry

    lax.fori_loop(0, count, drain, 0)
    for u in range(2):
        for g in range(nx):
            @pl.when(jnp.logical_not((gx == g) & (yz == 2 * gx + u)))
            def _():
                fourth(u * nx + g, u, g).wait_send()


def project(inputs, weight, nx, ny, call_id, head=False):
    rows, features = inputs.shape
    depth = features // nx
    part = depth // ny if head else depth
    width = weight.shape[1]
    wire = jnp.float32 if head else jnp.bfloat16
    limit = 256 if part > 2048 else 512
    tile = max(t for t in (128, 256, 512) if t <= limit and width % t == 0)
    count = width // tile
    group = 2 * nx * rows
    dma = pltpu.SemaphoreType.DMA
    blocks = inputs.reshape(rows, nx, depth).transpose(1, 0, 2)
    return pl.pallas_call(
        functools.partial(project_kernel, nx, ny, head, tile),
        out_shape=jax.ShapeDtypeStruct((rows, width if head else ny * width), wire),
        in_specs=[
            pl.BlockSpec(memory_space=pltpu.VMEM),
            pl.BlockSpec(memory_space=pl.ANY),
        ],
        out_specs=pl.BlockSpec(memory_space=pltpu.VMEM),
        scratch_shapes=[
            pltpu.VMEM((count, part, tile), jnp.bfloat16),
            pltpu.VMEM((nx, rows, depth), jnp.bfloat16),
            pltpu.VMEM((nx * rows, depth), jnp.float32),
            pltpu.VMEM((ny if head else 1, nx * rows, part), jnp.bfloat16),
            pltpu.VMEM((ny, nx * rows, part), jnp.bfloat16),
            pltpu.VMEM((ny * nx * rows, part), jnp.bfloat16),
            pltpu.VMEM((nx, group, width), wire),
            pltpu.VMEM((nx, group, width), wire),
            pltpu.VMEM((2 * nx, rows, width), wire),
            pltpu.VMEM((ny, rows, width), wire),
            dma((count,)),
            dma((nx,)),
            dma((nx,)),
            dma((ny,)),
            dma((ny,)),
            dma((count, nx)),
            dma((count, nx)),
            dma((2 * nx,)),
            dma((ny,)),
        ],
        compiler_params=pltpu.CompilerParams(
            collective_id=call_id, has_side_effects=True, vmem_limit_bytes=56 * 1024 * 1024
        ),
        cost_estimate=pl.CostEstimate(
            flops=2 * ny * nx * rows * part * width,
            bytes_accessed=2 * part * width,
            transcendentals=0,
        ),
    )(blocks, weight)


def attend(queries, k_cache, v_cache, lengths, keys_new, values_new):
    groups = HEADS // KV_HEADS
    factor = 1.0 / math.sqrt(HEAD)
    steps, rows_here = queries.shape[:2]
    cache_len = k_cache.shape[1]
    query_heads = queries.reshape(steps, rows_here, KV_HEADS, groups, HEAD)
    kcache_heads = k_cache.reshape(rows_here, cache_len, KV_HEADS, HEAD)
    vcache_heads = v_cache.reshape(rows_here, cache_len, KV_HEADS, HEAD)
    knew_heads = keys_new.reshape(steps, rows_here, KV_HEADS, HEAD)
    vnew_heads = values_new.reshape(steps, rows_here, KV_HEADS, HEAD)
    scores_cache = (
        jnp.einsum("srkgd,rlkd->srkgl", query_heads, kcache_heads, preferred_element_type=jnp.float32)
        * factor
    )
    valid = jnp.arange(cache_len)[None, None, None, None, :] < lengths[None, :, None, None, None]
    scores_cache = jnp.where(valid, scores_cache, -jnp.inf)
    scores_new = (
        jnp.einsum("srkgd,nrkd->srkgn", query_heads, knew_heads, preferred_element_type=jnp.float32)
        * factor
    )
    order = jnp.arange(steps)
    seen = (order[None, :] <= order[:, None])[:, None, None, None, :]
    scores_new = jnp.where(seen, scores_new, -jnp.inf)
    largest = jnp.maximum(jnp.max(scores_cache, -1), jnp.max(scores_new, -1))[..., None]
    exp_cache = jnp.where(valid, jnp.exp(scores_cache - largest), 0.0)
    exp_new = jnp.where(seen, jnp.exp(scores_new - largest), 0.0)
    denominator = jnp.sum(exp_cache, -1, keepdims=True) + jnp.sum(exp_new, -1, keepdims=True)
    weights_cache = (exp_cache / denominator).astype(jnp.bfloat16)
    weights_new = (exp_new / denominator).astype(jnp.bfloat16)
    result = jnp.einsum(
        "srkgl,rlkd->srkgd", weights_cache, vcache_heads, preferred_element_type=jnp.float32
    )
    result = result + jnp.einsum(
        "srkgn,nrkd->srkgd", weights_new, vnew_heads, preferred_element_type=jnp.float32
    )
    return result.reshape(steps * rows_here, HEADS * HEAD).astype(jnp.bfloat16)


def element_table(token_elem):
    return (token_elem[:, None] == jnp.arange(ELEMENTS, dtype=jnp.int32)[None, :]).astype(
        jnp.float32
    )


def masked_log_probs(logits, remaining, token_elem):
    element_hot = element_table(token_elem)
    per_token = jnp.dot(remaining, element_hot.T)
    allowed = (per_token > 0.5) | (token_elem == ELEMENTS)[None, :]
    largest = jnp.max(jnp.where(allowed, logits, -jnp.inf), -1, keepdims=True)
    shifted = logits - largest
    denominator = jnp.sum(jnp.where(allowed, jnp.exp(shifted), 0.0), -1, keepdims=True)
    return jnp.where(allowed, shifted - jnp.log(denominator), 0.0)


def used_elements(tokens, token_elem):
    token_hot = (tokens[:, None] == jnp.arange(VOCAB, dtype=jnp.int32)[None, :]).astype(jnp.float32)
    return jnp.dot(token_hot, element_table(token_elem))


def per_device(
    nx,
    ny,
    hidden_in,
    k_cache,
    v_cache,
    lengths,
    counts,
    token_elem,
    tokens,
    attn_gain,
    qkv_weight,
    o_weight,
    ffn_gain,
    gate_up_weight,
    down_weight,
    final_gain,
    lm_weight,
):
    q_width = HEADS * HEAD
    kv_width = KV_HEADS * HEAD
    steps, rows_here, width = hidden_in.shape
    layer_in = hidden_in.reshape(steps * rows_here, width)
    positions = (jnp.arange(steps, dtype=jnp.int32)[:, None] + lengths[None, :]).reshape(-1)
    mixed = project(norm_rows(layer_in, attn_gain), qkv_weight, nx, ny, 0)
    queries = rotate(mixed[:, :q_width].reshape(-1, HEADS, HEAD), positions)
    keys_now = rotate(
        mixed[:, q_width : q_width + kv_width].reshape(-1, KV_HEADS, HEAD), positions
    )
    values_now = mixed[:, q_width + kv_width :]
    attended = attend(
        queries.reshape(steps, rows_here, q_width),
        k_cache,
        v_cache,
        lengths,
        keys_now.reshape(steps, rows_here, kv_width),
        values_now.reshape(steps, rows_here, kv_width),
    )
    projected = project(attended, o_weight, nx, ny, 1)
    residual = (layer_in.astype(jnp.float32) + projected.astype(jnp.float32)).astype(jnp.bfloat16)
    gate_up = project(norm_rows(residual, ffn_gain), gate_up_weight, nx, ny, 2)
    hidden_units = (
        jax.nn.silu(gate_up[:, :FF].astype(jnp.float32)) * gate_up[:, FF:].astype(jnp.float32)
    ).astype(jnp.bfloat16)
    lowered = project(hidden_units, down_weight, nx, ny, 3)
    result = (residual.astype(jnp.float32) + lowered.astype(jnp.float32)).astype(jnp.bfloat16)
    logits = project(norm_rows(result, final_gain), lm_weight, nx, ny, 4, head=True)
    logit_steps = logits.reshape(steps, rows_here, VOCAB)
    outputs = result.reshape(steps, rows_here, width)
    remaining = counts.astype(jnp.float32)
    first_log = masked_log_probs(logit_steps[0], remaining, token_elem)
    remaining = remaining - used_elements(tokens, token_elem)
    second_log = masked_log_probs(logit_steps[1], remaining, token_elem)
    return (outputs, jnp.stack([first_log, second_log]))


def solution(mesh):
    return jax.shard_map(
        functools.partial(per_device, mesh.shape["gx"], mesh.shape["yz"]),
        mesh=mesh,
        in_specs=(
            P(None, ("gx", "yz"), None),
            P(("gx", "yz"), None, None),
            P(("gx", "yz"), None, None),
            P(("gx", "yz")),
            P(("gx", "yz"), None),
            P(),
            P(("gx", "yz")),
            P(),
            P("gx", "yz"),
            P("gx", "yz"),
            P(),
            P("gx", "yz"),
            P("gx", "yz"),
            P(),
            P(("gx", "yz"), None),
        ),
        out_specs=(P(None, ("gx", "yz"), None), P(None, ("gx", "yz"), None)),
        check_vma=False,
    )
```

```python
import functools
import math

import jax
import jax.numpy as jnp
from jax import lax
from jax.experimental import pallas as pl
from jax.experimental.pallas import tpu as pltpu
from jax.sharding import PartitionSpec as P

FF = 28672
HEADS = 64
KV_HEADS = 8
HEAD = 128
VOCAB = 512
ELEMENTS = 16


NORM_EPS = 1e-05
ROPE_THETA = 500000.0


def norm_rows(values, gain_vec):
    wide = values.astype(jnp.float32)
    inverse = lax.rsqrt(jnp.mean(wide * wide, axis=-1, keepdims=True) + NORM_EPS)
    return (wide * inverse * gain_vec).astype(jnp.bfloat16)


def rotate(heads_in, positions):
    half_width = heads_in.shape[-1] // 2
    frequency = jnp.power(
        ROPE_THETA, -(jnp.arange(half_width, dtype=jnp.float32) * 2.0 / heads_in.shape[-1])
    )
    angles = positions.astype(jnp.float32)[:, None] * frequency[None, :]
    cos_part = jnp.cos(angles)[:, None, :]
    sin_part = jnp.sin(angles)[:, None, :]
    wide = heads_in.astype(jnp.float32)
    first_half = wide[..., :half_width]
    second_half = wide[..., half_width:]
    joined = jnp.concatenate(
        [
            first_half * cos_part - second_half * sin_part,
            second_half * cos_part + first_half * sin_part,
        ],
        -1,
    )
    return joined.astype(jnp.bfloat16)


def project_kernel(
    nx,
    ny,
    head,
    tile,
    x_ref,
    w_ref,
    out_ref,
    wbuf,
    x1,
    strips,
    slot,
    xall,
    xmat,
    pbuf,
    rbuf,
    sbuf,
    obuf,
    wsem,
    ssem1,
    rsem1,
    ssem2,
    rsem2,
    ssem3,
    rsem3,
    ssem4,
    rsem4,
):
    gx = lax.axis_index("gx")
    yz = lax.axis_index("yz")
    count = wbuf.shape[0]
    rows = x1.shape[1]
    mesh_id = pl.DeviceIdType.MESH

    def fetch(c):
        cols = pl.ds(pl.multiple_of(c * tile, tile), tile)
        return pltpu.make_async_copy(w_ref.at[:, cols], wbuf.at[c], wsem.at[c])

    def begin(c, carry):
        fetch(c).start()
        return carry

    lax.fori_loop(0, count, begin, 0)

    home = yz // 2
    barrier = pltpu.get_barrier_semaphore()
    for d in range(1, nx):
        pl.semaphore_signal(
            barrier, inc=1, device_id=(lax.rem(gx + d, nx), yz), device_id_type=mesh_id
        )
    for d in range(1, ny):
        pl.semaphore_signal(
            barrier, inc=1, device_id=(gx, lax.rem(yz + d, ny)), device_id_type=mesh_id
        )
    for jj in range(ny):
        @pl.when(jnp.logical_not((home == gx) & (yz == jj)))
        def _():
            pl.semaphore_signal(barrier, inc=1, device_id=(home, jj), device_id_type=mesh_id)
    apart = (lax.rem(home + nx - gx, nx) + nx - 2) // (nx - 1)
    pl.semaphore_wait(barrier, nx - 1 + ny - 1 + ny - 1 + apart)

    def first(d):
        to = lax.rem(gx + d, nx)
        return pltpu.make_async_remote_copy(
            src_ref=x_ref.at[to],
            dst_ref=x1.at[gx],
            send_sem=ssem1.at[d],
            recv_sem=rsem1.at[d],
            device_id=(to, yz),
            device_id_type=mesh_id,
        )

    def first_in(d):
        return pltpu.make_async_remote_copy(
            src_ref=x_ref.at[gx],
            dst_ref=x1.at[lax.rem(gx + nx - d, nx)],
            send_sem=ssem1.at[d],
            recv_sem=rsem1.at[d],
            device_id=(lax.rem(gx + d, nx), yz),
            device_id_type=mesh_id,
        )

    for d in range(1, nx):
        first(d).start()
    x1[gx] = x_ref[gx]
    for d in range(1, nx):
        first_in(d).wait_recv()
    for g in range(nx):
        strips[g * rows : (g + 1) * rows, :] = x1[g].astype(jnp.float32)
    if head:
        width = xmat.shape[1]
        for jj in range(ny):
            slot[jj] = strips[:, jj * width : (jj + 1) * width].astype(jnp.bfloat16)
        xall[yz] = slot[yz]
    else:
        slot[0] = strips[...].astype(jnp.bfloat16)
        xall[yz] = slot[0]

    def second(d):
        to = lax.rem(yz + d, ny)
        return pltpu.make_async_remote_copy(
            src_ref=slot.at[to] if head else slot.at[0],
            dst_ref=xall.at[yz],
            send_sem=ssem2.at[d],
            recv_sem=rsem2.at[d],
            device_id=(gx, to),
            device_id_type=mesh_id,
        )

    def second_in(d):
        return pltpu.make_async_remote_copy(
            src_ref=slot.at[0],
            dst_ref=xall.at[lax.rem(yz + ny - d, ny)],
            send_sem=ssem2.at[d],
            recv_sem=rsem2.at[d],
            device_id=(gx, lax.rem(yz + d, ny)),
            device_id_type=mesh_id,
        )

    for d in range(1, ny):
        second(d).start()
    for d in range(1, ny):
        second_in(d).wait_recv()
    group = 2 * nx * rows
    for t in range(ny // 2):
        xmat[t * group : (t + 1) * group, :] = jnp.concatenate(
            [xall[2 * t].astype(jnp.float32), xall[2 * t + 1].astype(jnp.float32)], 0
        ).astype(jnp.bfloat16)

    def third(c, d):
        cols = pl.ds(pl.multiple_of(c * tile, tile), tile)
        to = lax.rem(gx + d, nx)
        return pltpu.make_async_remote_copy(
            src_ref=pbuf.at[to, :, cols],
            dst_ref=rbuf.at[d, :, cols],
            send_sem=ssem3.at[c, d],
            recv_sem=rsem3.at[c, d],
            device_id=(to, yz),
            device_id_type=mesh_id,
        )

    def multiply(c, carry):
        cols = pl.ds(pl.multiple_of(c * tile, tile), tile)
        fetch(c).wait()
        product = jnp.dot(xmat[...], wbuf[c], preferred_element_type=jnp.float32)
        for t in range(nx):
            pbuf[t, :, cols] = product[t * group : (t + 1) * group].astype(pbuf.dtype)
        for d in range(1, nx):
            third(c, d).start()
        return carry

    lax.fori_loop(0, count, multiply, 0)

    def reduce(c, carry):
        cols = pl.ds(pl.multiple_of(c * tile, tile), tile)
        for d in range(1, nx):
            third(c, d).wait_recv()
        total = pbuf[gx, :, cols].astype(jnp.float32)
        for d in range(1, nx):
            total = total + rbuf[d, :, cols].astype(jnp.float32)
        for k in range(2 * nx):
            sbuf[k, :, cols] = total[k * rows : (k + 1) * rows].astype(sbuf.dtype)
        return carry

    lax.fori_loop(0, count, reduce, 0)

    def fourth(k, u, g):
        return pltpu.make_async_remote_copy(
            src_ref=sbuf.at[k],
            dst_ref=obuf.at[yz],
            send_sem=ssem4.at[k],
            recv_sem=rsem4.at[yz],
            device_id=(g, 2 * gx + u),
            device_id_type=mesh_id,
        )

    def fourth_in(jj):
        return pltpu.make_async_remote_copy(
            src_ref=sbuf.at[0],
            dst_ref=obuf.at[jj],
            send_sem=ssem4.at[0],
            recv_sem=rsem4.at[jj],
            device_id=(lax.rem(gx + 1, nx), yz),
            device_id_type=mesh_id,
        )

    for u in range(2):
        for g in range(nx):
            mine = (gx == g) & (yz == 2 * gx + u)

            @pl.when(jnp.logical_not(mine))
            def _():
                fourth(u * nx + g, u, g).start()

            @pl.when(mine)
            def _():
                obuf[yz] = sbuf[u * nx + g]

    for jj in range(ny):
        @pl.when(jnp.logical_not((home == gx) & (yz == jj)))
        def _():
            fourth_in(jj).wait_recv()
    if head:
        out_ref[...] = sum(obuf[jj] for jj in range(ny))
    else:
        size = obuf.shape[2]
        for jj in range(ny):
            out_ref[:, jj * size : (jj + 1) * size] = obuf[jj]

    for d in range(1, nx):
        first(d).wait_send()
    for d in range(1, ny):
        second(d).wait_send()

    def drain(c, carry):
        for d in range(1, nx):
            third(c, d).wait_send()
        return carry

    lax.fori_loop(0, count, drain, 0)
    for u in range(2):
        for g in range(nx):
            @pl.when(jnp.logical_not((gx == g) & (yz == 2 * gx + u)))
            def _():
                fourth(u * nx + g, u, g).wait_send()


def project(inputs, weight, nx, ny, call_id, head=False):
    rows, features = inputs.shape
    depth = features // nx
    part = depth // ny if head else depth
    width = weight.shape[1]
    wire = jnp.float32 if head else jnp.bfloat16
    limit = 256 if part > 2048 else 512
    tile = max(t for t in (128, 256, 512) if t <= limit and width % t == 0)
    count = width // tile
    group = 2 * nx * rows
    dma = pltpu.SemaphoreType.DMA
    blocks = inputs.reshape(rows, nx, depth).transpose(1, 0, 2)
    return pl.pallas_call(
        functools.partial(project_kernel, nx, ny, head, tile),
        out_shape=jax.ShapeDtypeStruct((rows, width if head else ny * width), wire),
        in_specs=[
            pl.BlockSpec(memory_space=pltpu.VMEM),
            pl.BlockSpec(memory_space=pl.ANY),
        ],
        out_specs=pl.BlockSpec(memory_space=pltpu.VMEM),
        scratch_shapes=[
            pltpu.VMEM((count, part, tile), jnp.bfloat16),
            pltpu.VMEM((nx, rows, depth), jnp.bfloat16),
            pltpu.VMEM((nx * rows, depth), jnp.float32),
            pltpu.VMEM((ny if head else 1, nx * rows, part), jnp.bfloat16),
            pltpu.VMEM((ny, nx * rows, part), jnp.bfloat16),
            pltpu.VMEM((ny * nx * rows, part), jnp.bfloat16),
            pltpu.VMEM((nx, group, width), wire),
            pltpu.VMEM((nx, group, width), wire),
            pltpu.VMEM((2 * nx, rows, width), wire),
            pltpu.VMEM((ny, rows, width), wire),
            dma((count,)),
            dma((nx,)),
            dma((nx,)),
            dma((ny,)),
            dma((ny,)),
            dma((count, nx)),
            dma((count, nx)),
            dma((2 * nx,)),
            dma((ny,)),
        ],
        compiler_params=pltpu.CompilerParams(
            collective_id=call_id, has_side_effects=True, vmem_limit_bytes=56 * 1024 * 1024
        ),
        cost_estimate=pl.CostEstimate(
            flops=2 * ny * nx * rows * part * width,
            bytes_accessed=2 * part * width,
            transcendentals=0,
        ),
    )(blocks, weight)


def attend(queries, k_cache, v_cache, lengths, keys_new, values_new):
    groups = HEADS // KV_HEADS
    factor = 1.0 / math.sqrt(HEAD)
    steps, rows_here = queries.shape[:2]
    cache_len = k_cache.shape[1]
    query_heads = queries.reshape(steps, rows_here, KV_HEADS, groups, HEAD)
    kcache_heads = k_cache.reshape(rows_here, cache_len, KV_HEADS, HEAD)
    vcache_heads = v_cache.reshape(rows_here, cache_len, KV_HEADS, HEAD)
    knew_heads = keys_new.reshape(steps, rows_here, KV_HEADS, HEAD)
    vnew_heads = values_new.reshape(steps, rows_here, KV_HEADS, HEAD)
    scores_cache = (
        jnp.einsum("srkgd,rlkd->srkgl", query_heads, kcache_heads, preferred_element_type=jnp.float32)
        * factor
    )
    valid = jnp.arange(cache_len)[None, None, None, None, :] < lengths[None, :, None, None, None]
    scores_cache = jnp.where(valid, scores_cache, -jnp.inf)
    scores_new = (
        jnp.einsum("srkgd,nrkd->srkgn", query_heads, knew_heads, preferred_element_type=jnp.float32)
        * factor
    )
    order = jnp.arange(steps)
    seen = (order[None, :] <= order[:, None])[:, None, None, None, :]
    scores_new = jnp.where(seen, scores_new, -jnp.inf)
    largest = jnp.maximum(jnp.max(scores_cache, -1), jnp.max(scores_new, -1))[..., None]
    exp_cache = jnp.where(valid, jnp.exp(scores_cache - largest), 0.0)
    exp_new = jnp.where(seen, jnp.exp(scores_new - largest), 0.0)
    denominator = jnp.sum(exp_cache, -1, keepdims=True) + jnp.sum(exp_new, -1, keepdims=True)
    weights_cache = (exp_cache / denominator).astype(jnp.bfloat16)
    weights_new = (exp_new / denominator).astype(jnp.bfloat16)
    result = jnp.einsum(
        "srkgl,rlkd->srkgd", weights_cache, vcache_heads, preferred_element_type=jnp.float32
    )
    result = result + jnp.einsum(
        "srkgn,nrkd->srkgd", weights_new, vnew_heads, preferred_element_type=jnp.float32
    )
    return result.reshape(steps * rows_here, HEADS * HEAD).astype(jnp.bfloat16)


def element_table(token_elem):
    return (token_elem[:, None] == jnp.arange(ELEMENTS, dtype=jnp.int32)[None, :]).astype(
        jnp.float32
    )


def masked_log_probs(logits, remaining, token_elem):
    element_hot = element_table(token_elem)
    per_token = jnp.dot(remaining, element_hot.T)
    allowed = (per_token > 0.5) | (token_elem == ELEMENTS)[None, :]
    largest = jnp.max(jnp.where(allowed, logits, -jnp.inf), -1, keepdims=True)
    shifted = logits - largest
    denominator = jnp.sum(jnp.where(allowed, jnp.exp(shifted), 0.0), -1, keepdims=True)
    return jnp.where(allowed, shifted - jnp.log(denominator), 0.0)


def used_elements(tokens, token_elem):
    token_hot = (tokens[:, None] == jnp.arange(VOCAB, dtype=jnp.int32)[None, :]).astype(jnp.float32)
    return jnp.dot(token_hot, element_table(token_elem))


def per_device(
    nx,
    ny,
    hidden_in,
    k_cache,
    v_cache,
    lengths,
    counts,
    token_elem,
    tokens,
    attn_gain,
    qkv_weight,
    o_weight,
    ffn_gain,
    gate_up_weight,
    down_weight,
    final_gain,
    lm_weight,
):
    q_width = HEADS * HEAD
    kv_width = KV_HEADS * HEAD
    steps, rows_here, width = hidden_in.shape
    layer_in = hidden_in.reshape(steps * rows_here, width)
    positions = (jnp.arange(steps, dtype=jnp.int32)[:, None] + lengths[None, :]).reshape(-1)
    mixed = project(norm_rows(layer_in, attn_gain), qkv_weight, nx, ny, 0)
    queries = rotate(mixed[:, :q_width].reshape(-1, HEADS, HEAD), positions)
    keys_now = rotate(
        mixed[:, q_width : q_width + kv_width].reshape(-1, KV_HEADS, HEAD), positions
    )
    values_now = mixed[:, q_width + kv_width :]
    attended = attend(
        queries.reshape(steps, rows_here, q_width),
        k_cache,
        v_cache,
        lengths,
        keys_now.reshape(steps, rows_here, kv_width),
        values_now.reshape(steps, rows_here, kv_width),
    )
    projected = project(attended, o_weight, nx, ny, 1)
    residual = (layer_in.astype(jnp.float32) + projected.astype(jnp.float32)).astype(jnp.bfloat16)
    gate_up = project(norm_rows(residual, ffn_gain), gate_up_weight, nx, ny, 2)
    hidden_units = (
        jax.nn.silu(gate_up[:, :FF].astype(jnp.float32)) * gate_up[:, FF:].astype(jnp.float32)
    ).astype(jnp.bfloat16)
    lowered = project(hidden_units, down_weight, nx, ny, 3)
    result = (residual.astype(jnp.float32) + lowered.astype(jnp.float32)).astype(jnp.bfloat16)
    logits = project(norm_rows(result, final_gain), lm_weight, nx, ny, 4, head=True)
    outputs = result.reshape(steps, rows_here, width)
    first_left = counts.astype(jnp.float32)
    second_left = first_left - used_elements(tokens, token_elem)
    remaining = jnp.concatenate([first_left, second_left], 0)
    logs = masked_log_probs(logits, remaining, token_elem)
    return (outputs, logs.reshape(steps, rows_here, VOCAB))


def solution(mesh):
    return jax.shard_map(
        functools.partial(per_device, mesh.shape["gx"], mesh.shape["yz"]),
        mesh=mesh,
        in_specs=(
            P(None, ("gx", "yz"), None),
            P(("gx", "yz"), None, None),
            P(("gx", "yz"), None, None),
            P(("gx", "yz")),
            P(("gx", "yz"), None),
            P(),
            P(("gx", "yz")),
            P(),
            P("gx", "yz"),
            P("gx", "yz"),
            P(),
            P("gx", "yz"),
            P("gx", "yz"),
            P(),
            P(("gx", "yz"), None),
        ),
        out_specs=(P(None, ("gx", "yz"), None), P(None, ("gx", "yz"), None)),
        check_vma=False,
    )
```
